256 devices in a mesh: band: 32 (over y_lo, z, core), col: 8 (over x, y_hi).
Axes of the slice: x: 4, y: 4 (y_hi: 2, y_lo: 2; y = y_hi * 2 + y_lo), z: 8, core: 2. Of those that a mesh axis runs over, the one named last changes fastest.
Arguments:
- grad: float32 [16384, 8192], P('band', 'col'), as said below
Outputs:
- update: float32 [16384, 8192], P('band', 'col')
Inputs may be any that keep to these rules, and one draw needn't show every extreme that they name: `grad`: Real-valued gradient entries.
All inputs are finite; a program needn't handle non-finite values.
Results may differ from the reference program's by a relative error of at most 0.0003.
Values sent between devices are 32-bit elements; how exact they have to be, the bound alone decides.
No kernel may reach another device: no remote copies, remote signals or barrier semaphores. Data moves between devices by JAX's collectives and lax.ppermute only.
A program may use at most 64 MiB of HBM per device.

```python
import jax
import jax.numpy as jnp
from jax import lax

BAND = 512
COLS = 8192
ROWS = 16384


def draw_grad(key, part):
    key = jax.random.fold_in(key, 11)
    key_rows, key_cols, key_base = jax.random.split(key, 3)
    row_scale = jnp.exp(jax.random.uniform(key_rows, (ROWS, 1), jnp.float32) * jnp.log(10.0))
    col_scale = jnp.exp(jax.random.uniform(key_cols, (1, COLS), jnp.float32) * jnp.log(10.0))
    base = jnp.clip(jax.random.normal(key_base, (ROWS, COLS), jnp.float32), -4.0, 4.0)
    return (base * row_scale * col_scale / 3.0).astype(jnp.float32)


def setup_inputs(seed: int = 0) -> dict:
    streams_of = jax.random.split(jax.random.key(seed), 2)
    grad = draw_grad(jax.random.fold_in(streams_of[1], 71), 0)
    return dict(grad=grad)


damping = 0.1

def cho_apply(matrix, rhs):
    factor = jnp.linalg.cholesky(matrix)
    half = lax.linalg.triangular_solve(factor, rhs, left_side=True, lower=True)
    return lax.linalg.triangular_solve(factor, half, left_side=True, lower=True, transpose_a=True)

def reference(grad):
    count = ROWS // BAND
    blocks = grad.reshape(count, BAND, COLS)
    eye = jnp.eye(BAND, dtype=jnp.float32)
    high = lax.Precision.HIGHEST
    diag = jnp.einsum('bic,bjc->bij', blocks, blocks, precision=high) / COLS + damping * eye
    cross = jnp.einsum('bic,bjc->bij', blocks[:-1], blocks[1:], precision=high) / COLS
    coupling = jax.vmap(cho_apply)(diag[:-1], cross)
    schur = diag[1:] - jnp.einsum('bji,bjk->bik', cross, coupling, precision=high)
    schur_all = jnp.concatenate([diag[:1], schur], axis=0)
    lowered = blocks[1:] - jnp.einsum('bji,bjc->bic', coupling, blocks[:-1], precision=high)
    lowered_all = jnp.concatenate([blocks[:1], lowered], axis=0)
    solved = jax.vmap(cho_apply)(schur_all, lowered_all)
    tail = jnp.einsum('bij,bjc->bic', coupling, solved[1:], precision=high)
    result = solved.at[:-1].add(-tail)
    return result.reshape(ROWS, COLS)
```

```python
import jax
import jax.numpy as jnp
from jax import lax
from jax.experimental import pallas as pl
from jax.experimental.pallas import tpu as pltpu
from jax.sharding import PartitionSpec as P

f32, bf16 = jnp.float32, jnp.bfloat16
damping = 0.1
NN = (((1,), (0,)), ((), ()))
NT = (((1,), (1,)), ((), ()))


def dot1(left, right, dims=NN):
    return lax.dot_general(left, right, dims, preferred_element_type=f32)


def split(a):
    high = a.astype(bf16)
    return high, (a - high.astype(f32)).astype(bf16)


def dot3(left, right, dims=NN):
    (lh, ll), (rh, rl) = left, right
    return dot1(lh, rh, dims) + (dot1(lh, rl, dims) + dot1(ll, rh, dims))


def dot6(left, right, dims=NN):
    return lax.dot_general(
        left, right, dims, precision=lax.Precision.HIGHEST, preferred_element_type=f32
    )


def diagonal(n):
    rows = lax.broadcasted_iota(jnp.int32, (n, n), 0)
    return rows == lax.broadcasted_iota(jnp.int32, (n, n), 1)


def sweep_all(w_ref):
    n = w_ref.shape[0]
    lane = lax.broadcasted_iota(jnp.int32, (n, n), 1)
    sub = lax.broadcasted_iota(jnp.int32, (n, n), 0)
    along = lax.broadcasted_iota(jnp.int32, (1, n), 1)

    def sweep(j, carry):
        w = w_ref[...]
        row = w_ref[pl.ds(j, 1), :]
        col = jnp.sum(jnp.where(lane == j, w, 0.0), axis=1, keepdims=True)
        pivot = jnp.sum(jnp.where(along == j, row, 0.0), axis=1, keepdims=True)
        inv = 1.0 / pivot
        new = w - col * (row * inv)
        new = jnp.where(sub == j, row * inv, new)
        new = jnp.where(lane == j, col * inv, new)
        w_ref[...] = jnp.where(jnp.logical_and(sub == j, lane == j), -inv, new)
        return carry

    lax.fori_loop(0, n, sweep, 0)


def invert(a_ref, x_ref, s_ref, e_ref):
    n = a_ref.shape[0]
    on = diagonal(n)
    a = a_ref[...]
    d = jnp.where(on, a, 0.0)
    s_row = lax.rsqrt(jnp.sum(d, axis=0, keepdims=True))
    s_col = lax.rsqrt(jnp.sum(d, axis=1, keepdims=True))
    s = a * s_col * s_row
    s_ref[...] = s
    high = s.astype(bf16)
    s2 = dot1(high, high)
    bound = jnp.sqrt(jnp.max(jnp.sum(jnp.abs(s2), axis=1, keepdims=True))) * 1.02
    alpha = 1.9 / bound
    e_ref[...] = jnp.where(on, 1.0, 0.0) - (2 * alpha) * s + (alpha * alpha) * s2
    x_ref[...] = jnp.where(on, 2 * alpha, 0.0) - (alpha * alpha) * s

    def unsettled(state):
        step, size = state
        return jnp.logical_and(step < 14, size > 0.1)

    def square(state):
        step, _ = state
        e = e_ref[...].astype(bf16)
        x = x_ref[...]
        x_ref[...] = x + dot1(x.astype(bf16), e)
        e = dot1(e, e)
        e_ref[...] = e
        return step + 1, jnp.sum(e * e)

    lax.while_loop(unsettled, square, (0, jnp.float32(1.0)))

    def rough(state):
        step, size = state
        return jnp.logical_and(step < 5, size > 1e-4)

    def refine(state):
        step, _ = state
        x = x_ref[...]
        r = jnp.where(on, 1.0, 0.0) - dot3(split(s_ref[...]), split(x))
        x_ref[...] = x + dot1(x.astype(bf16), r.astype(bf16))
        return step + 1, jnp.sum(r * r)

    lax.while_loop(rough, refine, (0, jnp.float32(1.0)))
    x = x_ref[...]
    r = jnp.where(on, 1.0, 0.0) - dot6(s_ref[...], x)
    x_ref[...] = (x + dot1(x.astype(bf16), r.astype(bf16))) * s_col * s_row

    @pl.when(jnp.logical_not(jnp.sum(r * r) < 1e-6))
    def _():
        s_ref[...] = a_ref[...]
        sweep_all(s_ref)
        x_ref[...] = -s_ref[...]


VMEM = pl.BlockSpec(memory_space=pltpu.VMEM)
PARAMS = pltpu.CompilerParams(vmem_limit_bytes=50 << 20)


def inverse(a):
    n = a.shape[0]
    return pl.pallas_call(
        invert,
        out_shape=jax.ShapeDtypeStruct((n, n), f32),
        in_specs=[VMEM],
        out_specs=VMEM,
        scratch_shapes=[pltpu.VMEM((n, n), f32)] * 2,
        compiler_params=PARAMS,
    )(a)


def solve_kernel(x_ref, ct_ref, h_ref, below_ref, above_ref, kt_ref, z_ref, a_ref, xs_ref, s_ref, e_ref):
    ct = split(ct_ref[...])
    kt_ref[...] = dot3(ct, split(x_ref[...]))
    kt = split(kt_ref[...])
    a_ref[...] = h_ref[...] - dot3(kt, ct, NT)
    invert(a_ref, xs_ref, s_ref, e_ref)
    y = above_ref[...] - dot3(kt, split(below_ref[...]))
    z_ref[...] = dot3(split(xs_ref[...]), split(y))


def solve(x, ct, h, below, above):
    n, m = above.shape
    return pl.pallas_call(
        solve_kernel,
        out_shape=[jax.ShapeDtypeStruct((n, n), f32), jax.ShapeDtypeStruct((n, m), f32)],
        in_specs=[VMEM] * 5,
        out_specs=[VMEM] * 2,
        scratch_shapes=[pltpu.VMEM((n, n), f32)] * 4,
        compiler_params=PARAMS,
    )(x, ct, h, below, above)


def handed(block, distance):
    n = lax.axis_size("band")
    return lax.ppermute(block, "band", [(i, (i + distance) % n) for i in range(n)])


def gram(left, right):
    return lax.dot_general(left, right, NT, precision=lax.Precision.HIGH)


def summed(part, scale):
    count = lax.axis_size("col")
    rows, cols = part.shape
    stripes = lax.all_to_all(part.reshape(count, rows // count, cols), "col", 0, 0)
    stripe = stripes.sum(0) * scale
    every = jnp.broadcast_to(stripe[None], stripes.shape)
    return lax.all_to_all(every, "col", 0, 0).reshape(rows, cols)


def local(grad):
    rows = grad.shape[0]
    total_cols = grad.shape[1] * lax.axis_size("col")
    band, bands = lax.axis_index("band"), lax.axis_size("band")
    above = handed(grad, -1)
    own = summed(gram(grad, grad), 1.0 / total_cols) + damping * jnp.eye(rows, dtype=f32)
    last = band == bands - 1
    cross_t = summed(gram(above, grad), jnp.where(last, 0.0, 1.0 / total_cols))
    own_above = handed(own, -1)
    kt, solved = solve(inverse(own), cross_t, own_above, grad, above)
    mine = handed(solved, 1)
    tail = lax.dot_general(kt, solved, (((0,), (0,)), ((), ())), precision=lax.Precision.HIGH)
    return mine - tail


def solution(mesh):
    return jax.shard_map(
        local,
        mesh=mesh,
        in_specs=(P("band", "col"),),
        out_specs=P("band", "col"),
        check_vma=False,
    )
```
